128 devices in a mesh: lon: 16 (over x, z), lat: 2 (over y_lo), mem: 4 (over y_hi, core).
Axes of the slice: x: 4, y: 4 (y_hi: 2, y_lo: 2; y = y_hi * 2 + y_lo), z: 4, core: 2. Of those that a mesh axis runs over, the one named last changes fastest.
Arguments:
- perturb: float32 [8, 2, 2048, 4096], P('mem', None, 'lat', 'lon'), may hold values from -6 to 6
- control: float32 [8, 2, 2048, 4096], P('mem', None, 'lat', 'lon'), may hold values from -6 to 6
- diffusivity: float32 [2048, 4096], P('lat', 'lon'), may hold values from 0.05 to 0.24
- sea_mask: int32 [2, 2048, 4096], P(None, 'lat', 'lon'), may hold values 0 or 1
- fold_partner: int32 [4096], replicated, may hold values from 0 to 4095, as said below
Outputs:
- increment: float32 [2, 2048, 4096], P(None, 'lat', 'lon')
The draws below stay inside these ranges and needn't reach their ends.
Inputs may be any that keep to these rules, and one draw needn't show every extreme that they name: `sea_mask`: 1 marks sea and 0 land. fold_partner[i] = (2 p - 1 - i) mod 4096 for a fold pivot column p of the case; it is its own inverse and never maps a column to itself.
All inputs are finite; a program needn't handle non-finite values. No bound on the sum of `sea_mask` on one device may be relied on, other than what follows from the above.
Results may differ from the reference program's by a relative error of at most 0.00002.
Values sent between devices are 32-bit elements; how exact they have to be, the bound alone decides.
No kernel may reach another device: no remote copies, remote signals or barrier semaphores. Data moves between devices by JAX's collectives and lax.ppermute only.
A program may use at most 192 MiB of HBM per device.

```python
import math
import jax
import jax.numpy as jnp
from jax import lax

LEV = 2
PASSES = 3
MEMBERS = 8
LON = 4096
LAT = 2048


def draw_fold_partner(key, part):
    key = jax.random.fold_in(key, 11)
    fold_pivot = jax.random.randint(key, (), 0, LON, dtype=jnp.int32)
    col_ids = jnp.arange(LON, dtype=jnp.int32)
    return jnp.mod(2 * fold_pivot - 1 - col_ids, LON).astype(jnp.int32)


def plant(values, stream_key, smallest, largest):
    longest = values.shape.index(max(values.shape))
    spots = []
    for shift in (0, 1):
        where = [jax.random.randint(jax.random.fold_in(stream_key, axis), (), 0, length) for axis, length in enumerate(values.shape)]
        where[longest] = (where[longest] + shift) % values.shape[longest]
        spots.append(tuple(where))
    return values.at[spots[0]].set(smallest).at[spots[1]].set(largest)


def shard_levels(key, shape, cuts, least, largest):
    def one(dim, shards_of):
        draws = jax.random.uniform(jax.random.fold_in(jax.random.fold_in(key, 6), dim), (shards_of,), jnp.float32, least / len(cuts), largest / len(cuts))
        return jnp.repeat(jnp.exp(draws), shape[dim] // shards_of).reshape((-1,) + (1,) * (len(shape) - dim - 1))

    gain = one(*cuts[0])
    for cut in cuts[1:]:
        gain = gain * one(*cut)
    return gain


def gaussian(key, shape, scale, limit, cuts=(), kind=jnp.bfloat16):
    gain = shard_levels(key, shape, cuts, -0.22, 0.18) if cuts else 1.0
    drawn = jax.random.normal(key, shape, jnp.float32) * scale * gain
    return jnp.minimum(jnp.maximum(drawn, -limit), limit).astype(kind)


def setup_inputs(seed: int = 0) -> dict:
    key_list = jax.random.split(jax.random.key(seed), 6)
    return {
        "perturb": gaussian(key_list[0], (MEMBERS, LEV, LAT, LON), 1.0, 6.0, ((0, 4), (2, 2), (3, 16)), jnp.float32),
        "control": gaussian(key_list[1], (MEMBERS, LEV, LAT, LON), 1.0, 6.0, ((0, 4), (2, 2), (3, 16)), jnp.float32),
        "diffusivity": jnp.clip(jnp.exp(math.log(0.24) - 1.5686159 * jax.random.uniform(key_list[2], (LAT, LON), jnp.float32) ** shard_levels(key_list[2], (LAT, LON), ((0, 2), (1, 16)), -0.2, 0.2)), 0.05, 0.24),
        "sea_mask": plant((jax.random.randint(key_list[3], (LEV, LAT, LON), 0, 10) < 7).astype(jnp.int32), jax.random.fold_in(key_list[3], 1), 0, 1),
        "fold_partner": draw_fold_partner(jax.random.fold_in(key_list[5], 71), 0),
    }


def extend(values, fold_partner):
    north_row = jnp.take(values[..., -1:, :], fold_partner, axis=-1)
    south_row = jnp.zeros_like(values[..., :1, :])
    stacked = jnp.concatenate([south_row, values, north_row], axis=-2)
    return jnp.concatenate([stacked[..., -1:], stacked, stacked[..., :1]], axis=-1)


def diffuse(current, kappa_pad, sea_pad):
    inner_rows = current.shape[-2] - 2
    inner_cols = current.shape[-1] - 2
    centre = current[..., 1:-1, 1:-1]
    kappa_mid = kappa_pad[1:-1, 1:-1]
    sea_mid = sea_pad[..., 1:-1, 1:-1]
    change = jnp.zeros_like(centre)
    for row_off, col_off in ((1, 2), (1, 0), (2, 1), (0, 1)):
        nearby = current[..., row_off:row_off + inner_rows, col_off:col_off + inner_cols]
        kappa_near = kappa_pad[row_off:row_off + inner_rows, col_off:col_off + inner_cols]
        sea_near = sea_pad[..., row_off:row_off + inner_rows, col_off:col_off + inner_cols]
        conduct = 0.5 * (kappa_mid + kappa_near) * sea_mid * sea_near
        change = change + conduct * (nearby - centre)
    return centre + change


def reference(perturb, control, diffusivity, sea_mask, fold_partner):
    sea_float = sea_mask.astype(jnp.float32)
    kappa_pad = extend(diffusivity, fold_partner)
    sea_pad = extend(sea_float, fold_partner)

    def member(running, member_pair):
        spread_field, weights_field = member_pair
        smooth = weights_field
        for sweep in range(PASSES):
            smooth = diffuse(extend(smooth, fold_partner), kappa_pad, sea_pad)
        return running + spread_field * smooth, None

    start = jnp.zeros((LEV, LAT, LON), jnp.float32)
    summed, unused = lax.scan(member, start, (perturb, control))
    return summed * sea_float
```

```python
import functools

import jax
import jax.numpy as jnp
from jax import lax
from jax.experimental import pallas as pl
from jax.experimental.pallas import tpu as pltpu
from jax.sharding import PartitionSpec as P

PASSES = 3
LANES = 128
TILE = 8
FIELDS = 7
PITCH = 16
GROUPS = 5
STEP = 16
F32 = jnp.float32
MIB = 1 << 20


def lane_ids(rows):
    return lax.broadcasted_iota(jnp.int32, (rows, LANES), 1)


def spin(value, shift):
    shift %= LANES
    return value if shift == 0 else pltpu.roll(value, shift, 1)


def east_of(tiles):
    turned = [spin(v, -1) for v in tiles]
    last = lane_ids(tiles[0].shape[0]) == LANES - 1
    return [
        jnp.where(last, turned[t + 1], turned[t]) if t + 1 < len(tiles) else turned[t]
        for t in range(len(tiles))
    ]


def west_of(tiles):
    turned = [spin(v, 1) for v in tiles]
    first = lane_ids(tiles[0].shape[0]) == 0
    return [jnp.where(first, turned[t - 1], turned[t]) if t else turned[t] for t in range(len(tiles))]


def conductances(kappa, sea, diag, g_east, g_west, g_north, low, high):
    tiles = range(kappa.shape[0])
    for r in range(low, high, STEP):
        k = [kappa[t, r : r + STEP, :] for t in tiles]
        s = [sea[t, r : r + STEP, :].astype(F32) for t in tiles]
        k_east, s_east = east_of(k), east_of(s)
        east = [0.5 * (k[t] + k_east[t]) * s[t] * s_east[t] for t in tiles]
        west = west_of(east)
        for t in tiles:
            k_n, s_n = kappa[t, r + 1 : r + STEP + 1, :], sea[t, r + 1 : r + STEP + 1, :].astype(F32)
            k_s, s_s = kappa[t, r - 1 : r + STEP - 1, :], sea[t, r - 1 : r + STEP - 1, :].astype(F32)
            north = 0.5 * (k[t] + k_n) * s[t] * s_n
            south = 0.5 * (k[t] + k_s) * s[t] * s_s
            diag[t, r : r + STEP, :] = 1.0 - ((east[t] + west[t]) + (north + south))
            g_east[t, r : r + STEP, :] = east[t]
            g_west[t, r : r + STEP, :] = west[t]
            g_north[t, r : r + STEP, :] = north


def diffused(field, coefs, r, member):
    diag, g_east, g_west, g_north = coefs
    tiles = range(diag.shape[0])
    here = [field[member, t, r : r + STEP, :] for t in tiles]
    east, west = east_of(here), west_of(here)
    out = []
    for t in tiles:
        north = field[member, t, r + 1 : r + STEP + 1, :]
        south = field[member, t, r - 1 : r + STEP - 1, :]
        out.append(
            (diag[t, r : r + STEP, :] * here[t])
            + (g_east[t, r : r + STEP, :] * east[t] + g_west[t, r : r + STEP, :] * west[t])
            + (g_north[t, r : r + STEP, :] * north + g_north[t, r - 1 : r + STEP - 1, :] * south)
        )
    return out


def sweep(source, target, coefs, low, high):
    for r in range(low, high, STEP):
        for member in range(source.shape[0]):
            for t, value in enumerate(diffused(source, coefs, r, member)):
                target[member, t, r : r + STEP, :] = value


def started(copies):
    for copy in copies:
        copy.start()
    return copies


def finish(copies):
    for copy in copies:
        copy.wait()


def band_kernel(keep, low, rows, has_rim, core, control, perturb, kappa, mask, *rest):
    rest = list(rest)
    rim = rest.pop(0) if has_rim else None
    other = rest.pop(0) if keep else None
    out, c_buf, v_buf, p_buf, k_buf, s_buf, diag, g_east, g_west, g_north, sems = rest
    level = core[0] if keep else 1 - core[0]
    total = control.shape[2]
    first, last = max(low - TILE, 0), min(low + rows + TILE, total)
    at = first - low + 2 * TILE
    count = last - first
    sem = iter(range(sems.shape[0]))
    early, late = [], []
    for t in range(2):
        cols = pl.ds(t * LANES, LANES)
        span, put = pl.ds(first, count), pl.ds(at, count)
        early.append(pltpu.make_async_copy(kappa.at[span, cols], k_buf.at[t, put], sems.at[next(sem)]))
        early.append(pltpu.make_async_copy(mask.at[level, span, cols], s_buf.at[t, put], sems.at[next(sem)]))
    for m in range(2):
        for t in range(2):
            cols = pl.ds(t * LANES, LANES)
            late.append(
                pltpu.make_async_copy(
                    control.at[m, level, pl.ds(first, count), cols],
                    c_buf.at[m, t, pl.ds(at, count)],
                    sems.at[next(sem)],
                )
            )
    for m in range(2):
        for t in range(2):
            cols = pl.ds(t * LANES, LANES)
            late.append(
                pltpu.make_async_copy(
                    perturb.at[m, level, pl.ds(low, rows), cols], p_buf.at[m, t], sems.at[next(sem)]
                )
            )
    started(early)
    started(late)
    finish(early)
    top = rows + 3 * TILE
    coefs = (diag, g_east, g_west, g_north)
    conductances(k_buf, s_buf, *coefs, TILE, top)
    finish(late)
    sweep(c_buf, v_buf, coefs, TILE, top)
    sweep(v_buf, c_buf, coefs, TILE, top)
    for r in range(2 * TILE, rows + 2 * TILE, STEP):
        one, two = (diffused(c_buf, coefs, r, m) for m in range(2))
        for t in range(2):
            q = r - 2 * TILE
            value = one[t] * p_buf[0, t, q : q + STEP, :] + two[t] * p_buf[1, t, q : q + STEP, :]
            value = value * s_buf[t, r : r + STEP, :].astype(F32)
            w = t * rows + q
            if keep:
                value = value + other[w : w + STEP, :]
            out[w : w + STEP, :] = value
    if has_rim:
        value = rim[...]
        if keep:
            value = value + other[2 * rows :, :]
        out[2 * rows :, :] = value


def band(keep, low, rows, core, control, perturb, kappa, mask, rim=None, other=None):
    extra = 0 if rim is None else rim.shape[0]
    operands = [core, control, perturb, kappa, mask]
    specs = [pl.BlockSpec(memory_space=pltpu.SMEM)] + [pl.BlockSpec(memory_space=pl.ANY)] * 4
    for value in (rim, other):
        if value is not None:
            operands.append(value)
            specs.append(pl.BlockSpec(memory_space=pltpu.VMEM))
    high = rows + 4 * TILE
    return pl.pallas_call(
        functools.partial(band_kernel, keep, low, rows, rim is not None),
        out_shape=jax.ShapeDtypeStruct((2 * rows + extra, LANES), F32),
        in_specs=specs,
        out_specs=pl.BlockSpec(memory_space=pltpu.VMEM),
        scratch_shapes=[
            pltpu.VMEM((2, 2, high, LANES), F32),
            pltpu.VMEM((2, 2, high, LANES), F32),
            pltpu.VMEM((2, 2, rows, LANES), F32),
            pltpu.VMEM((2, high, LANES), F32),
            pltpu.VMEM((2, high, LANES), jnp.int32),
        ]
        + [pltpu.VMEM((2, high, LANES), F32)] * 4
        + [pltpu.SemaphoreType.DMA((12,))],
        compiler_params=pltpu.CompilerParams(vmem_limit_bytes=24 * MIB),
        cost_estimate=pl.CostEstimate(flops=rows * 256 * 200, bytes_accessed=rows * 256 * 32, transcendentals=0),
        name="band_keep" if keep else "band_send",
    )(*operands)


def edge_kernel(place, c_low, c_high, k_low, k_high, s_low, s_high, low, high, message):
    for c, k, s, out in ((c_low, k_low, s_low, low), (c_high, k_high, s_high, high)):
        for m in range(2):
            for v in range(2):
                out[2 * m + v] = c[m, v]
        out[4] = k[...]
        out[5] = s[0].astype(F32)
        out[6] = s[1].astype(F32)
    message[...] = jnp.where(place[0] == 0, high[...], low[...])


def edges(place, control, kappa, mask):
    rows, cols = kappa.shape
    end = rows // TILE - 1
    shape = jax.ShapeDtypeStruct((FIELDS, TILE, cols), F32)
    specs = [pl.BlockSpec(memory_space=pltpu.SMEM)]
    specs += [pl.BlockSpec((2, 2, TILE, cols), lambda i, b=b: (0, 0, b, 0)) for b in (0, end)]
    specs += [pl.BlockSpec((TILE, cols), lambda i, b=b: (b, 0)) for b in (0, end)]
    specs += [pl.BlockSpec((2, TILE, cols), lambda i, b=b: (0, b, 0)) for b in (0, end)]
    return pl.pallas_call(
        edge_kernel,
        grid=(1,),
        out_shape=[shape] * 3,
        in_specs=specs,
        out_specs=[pl.BlockSpec((FIELDS, TILE, cols), lambda i: (0, 0, 0))] * 3,
        compiler_params=pltpu.CompilerParams(vmem_limit_bytes=8 * MIB),
        name="edge_rows",
    )(place, control, control, kappa, kappa, mask, mask)


def strips(left, right):
    rows = left[0].shape[0]
    lane = lane_ids(rows)
    west, east = jnp.zeros((rows, LANES), F32), jnp.zeros((rows, LANES), F32)
    for f in range(FIELDS):
        base = PITCH * f
        inside = jnp.logical_and(lane >= base + 3, lane < base + 9)
        west = jnp.where(inside, spin(left[f], base + 3), west)
        inside = jnp.logical_and(lane >= base, lane < base + 6)
        east = jnp.where(inside, spin(right[f], base - (LANES - 6)), east)
    return west, east


def strip_kernel(place, control, kappa, mask, low_rows, fold_a, fold_b, west, east, to_east, to_west, south, north,
                 c_buf, k_buf, s_buf, sems):
    rows = kappa.shape[0]
    parts = 4
    size = rows // parts
    copies = []
    for i in range(parts):
        span = pl.ds(i * size, size)
        copies.append(
            [
                pltpu.make_async_copy(control.at[:, :, span], c_buf.at[:, :, span], sems.at[3 * i]),
                pltpu.make_async_copy(kappa.at[span], k_buf.at[span], sems.at[3 * i + 1]),
                pltpu.make_async_copy(mask.at[:, span], s_buf.at[:, span], sems.at[3 * i + 2]),
            ]
        )
    for part in copies:
        started(part)
    bottom = place[0] == 0
    shift = place[1]
    lane = lane_ids(TILE)
    for f in range(FIELDS):
        south[f] = jnp.where(bottom, 0.0, low_rows[f])
        blocks = []
        for source in (fold_b, fold_a):
            for t in range(2):
                tile = source[f, :, t * LANES : (t + 1) * LANES]
                blocks.append(jnp.concatenate([tile[TILE - 1 - r : TILE - r] for r in range(TILE)], axis=0))
        for t in range(2):
            wanted = 2 * LANES + shift - t * LANES - lane
            inner, outer = wanted % LANES, wanted // LANES
            ghost = jnp.zeros((TILE, LANES), F32)
            for n, block in enumerate(blocks):
                turned = jnp.take_along_axis(block, inner, axis=1, mode="promise_in_bounds")
                ghost = jnp.where(outer == n, turned, ghost)
            part = slice(t * LANES, (t + 1) * LANES)
            north[f, :, part] = jnp.where(bottom, low_rows[f, :, part], ghost)
    for at, source in ((0, south), (rows + TILE, north)):
        left, right = strips(
            [source[f, :, :LANES] for f in range(FIELDS)], [source[f, :, LANES:] for f in range(FIELDS)]
        )
        west[at : at + TILE, :] = left
        east[at : at + TILE, :] = right
    for i in range(parts):
        finish(copies[i])
        for r in range(i * size, (i + 1) * size, STEP):
            halves = []
            for t in range(2):
                part = slice(t * LANES, (t + 1) * LANES)
                values = [c_buf[m, v, r : r + STEP, part] for m in range(2) for v in range(2)]
                values.append(k_buf[r : r + STEP, part])
                values += [s_buf[v, r : r + STEP, part].astype(F32) for v in range(2)]
                halves.append(values)
            left, right = strips(*halves)
            west[r + TILE : r + TILE + STEP, :] = left
            east[r + TILE : r + TILE + STEP, :] = right
    tiles = (rows + 2 * TILE) // TILE // GROUPS
    phase = lane % PITCH
    for source, target in ((east, to_east), (west, to_west)):
        for k in range(tiles):
            value = jnp.zeros((TILE, LANES), F32)
            for g in range(GROUPS):
                r = (g * tiles + k) * TILE
                inside = jnp.logical_and(phase >= 3 * g, phase < 3 * g + 3)
                value = jnp.where(inside, spin(source[r : r + TILE, :], 3 * g - 3), value)
            target[k * TILE : (k + 1) * TILE, :] = value


def pack_strips(place, control, kappa, mask, low_rows, fold_a, fold_b):
    rows, cols = kappa.shape
    tall = rows + 2 * TILE
    vmem = pl.BlockSpec(memory_space=pltpu.VMEM)
    anywhere = pl.BlockSpec(memory_space=pl.ANY)
    return pl.pallas_call(
        strip_kernel,
        out_shape=[jax.ShapeDtypeStruct((tall, LANES), F32)] * 2
        + [jax.ShapeDtypeStruct((tall // GROUPS, LANES), F32)] * 2
        + [jax.ShapeDtypeStruct((FIELDS, TILE, cols), F32)] * 2,
        in_specs=[pl.BlockSpec(memory_space=pltpu.SMEM)] + [anywhere] * 3 + [vmem] * 3,
        out_specs=[vmem] * 6,
        scratch_shapes=[
            pltpu.VMEM((2, 2, rows, cols), F32),
            pltpu.VMEM((rows, cols), F32),
            pltpu.VMEM((2, rows, cols), jnp.int32),
            pltpu.SemaphoreType.DMA((12,)),
        ],
        compiler_params=pltpu.CompilerParams(vmem_limit_bytes=24 * MIB),
        name="pack_strips",
    )(place, control, kappa, mask, low_rows, fold_a, fold_b)


def rim_kernel(core, west_in, east_in, from_west, from_east, low, high, south, north, perturb, keep, send,
               field, spare, kappa, mask, diag, g_east, g_west, g_north, r_field, r_spare, r_kappa, r_mask,
               r_diag, r_east, r_west, r_north, p_buf, sems):
    rows = perturb.shape[2]
    tall = rows + 2 * TILE
    copies = [
        pltpu.make_async_copy(perturb.at[m, v], p_buf.at[m, v], sems.at[2 * m + v]) for m in range(2) for v in range(2)
    ]
    started(copies)
    made = []
    for side, (under, over) in enumerate(((south, low), (high, north))):
        for t in range(2):
            part = slice(t * LANES, (t + 1) * LANES)
            for half, source in enumerate((under, over)):
                at = slice(TILE * (1 + half), TILE * (2 + half))
                for f in range(4):
                    r_field[2 * side + f % 2, f // 2, t, at, :] = source[f, :, part]
                r_kappa[side, t, at, :] = source[4, :, part]
                for v in range(2):
                    r_mask[2 * side + v, t, at, :] = source[5 + v, :, part]
        for v in range(2):
            n = 2 * side + v
            coefs = tuple(ref.at[n] for ref in (r_diag, r_east, r_west, r_north))
            conductances(r_kappa.at[side], r_mask.at[n], *coefs, TILE, 3 * TILE)
            sweep(r_field.at[n], r_spare.at[n], coefs, TILE, 3 * TILE)
            sweep(r_spare.at[n], r_field.at[n], coefs, TILE, 3 * TILE)
            sweep(r_field.at[n], r_spare.at[n], coefs, TILE, 3 * TILE)
    tiles = tall // TILE // GROUPS
    lane = lane_ids(TILE)
    phase = lane % PITCH
    strip = lane // PITCH
    for side, (own, message, at) in enumerate(((west_in, from_west, 0), (east_in, from_east, 6))):
        inside = jnp.logical_and(phase >= at, phase < at + 3)
        for i in range(tall // TILE):
            g, k = i // tiles, i % tiles
            value = jnp.where(
                inside, spin(message[k * TILE : (k + 1) * TILE, :], at - 3 * g), own[i * TILE : (i + 1) * TILE, :]
            )
            put = slice((i + 1) * TILE, (i + 2) * TILE)
            field[side, 0, 0, put, :] = value
            spread = spin(value, -4 * PITCH)
            for f in range(1, 4):
                spread = jnp.where(strip == f, spin(value, (f - 4) * PITCH), spread)
            kappa[side, 0, put, :] = spread
            mask[side, 0, put, :] = jnp.where(strip < 2, spin(value, -5 * PITCH), spin(value, -3 * PITCH))
        coefs = tuple(ref.at[side] for ref in (diag, g_east, g_west, g_north))
        conductances(kappa.at[side], mask.at[side], *coefs, TILE, tall + TILE)
        sweep(field.at[side], spare.at[side], coefs, TILE, tall + TILE)
        sweep(spare.at[side], field.at[side], coefs, TILE, tall + TILE)
    finish(copies)
    mine = core[0] == 0

    def give(at, value):
        put = slice(at, at + TILE)
        keep[put, :] = jnp.where(mine, value[0], value[1])
        send[put, :] = jnp.where(mine, value[1], value[0])

    def product(side, r):
        coefs = tuple(ref.at[side] for ref in (diag, g_east, g_west, g_north))
        value = diffused(field.at[side], coefs, r + 2 * TILE, 0)[0]
        value = value * mask[side, 0, r + 2 * TILE : r + 2 * TILE + STEP, :]
        weight = jnp.zeros((STEP, LANES), F32)
        wide = lane_ids(STEP)
        part = slice(LANES, 2 * LANES) if side else slice(0, LANES)
        for f in range(4):
            base = PITCH * f
            source = p_buf[f // 2, f % 2, r : r + STEP, part]
            weight = jnp.where(
                jnp.logical_and(wide >= base + 3, wide < base + 6),
                spin(source, base + 3 - (LANES - 3 if side else 0)),
                weight,
            )
        value = value * weight
        return value + spin(value, -2 * PITCH)

    groups = LANES // TILE
    block = rows // groups
    for r in range(0, block, STEP):
        values = [jnp.zeros((STEP, LANES), F32) for _ in range(2)]
        wide = lane_ids(STEP)
        for g in range(groups):
            for side in range(2):
                value = product(side, g * block + r)
                at = TILE * g + 5 * side
                inside = jnp.logical_and(wide >= at, wide < at + 3)
                for v in range(2):
                    values[v] = jnp.where(inside, spin(value, at - 3 - PITCH * v), values[v])
        for half in range(0, STEP, TILE):
            give(r + half, [value[half : half + TILE] for value in values])
    south_part = lax.broadcasted_iota(jnp.int32, (TILE, LANES), 0) < TILE // 2
    for t in range(2):
        part = slice(t * LANES, (t + 1) * LANES)
        values = []
        for v in range(2):
            ends = []
            for side, (r, at) in enumerate(((0, TILE * 2), (rows - TILE, TILE))):
                n = 2 * side + v
                total = sum(r_spare[n, m, t, at : at + TILE, :] * p_buf[m, v, r : r + TILE, part] for m in range(2))
                ends.append(total * r_mask[n, t, at : at + TILE, :])
            values.append(jnp.where(south_part, ends[0], ends[1]))
        give(block + TILE * t, values)


def rim_sums(core, west, east, from_west, from_east, low, high, south, north, perturb):
    rows, cols = perturb.shape[2:]
    tall = rows + 4 * TILE
    size = rows * TILE // LANES + 2 * TILE
    vmem = pl.BlockSpec(memory_space=pltpu.VMEM)
    strip = pltpu.VMEM((2, 1, tall, LANES), F32)
    row = pltpu.VMEM((4, 2, 4 * TILE, LANES), F32)
    return pl.pallas_call(
        rim_kernel,
        out_shape=[jax.ShapeDtypeStruct((size, LANES), F32)] * 2,
        in_specs=[pl.BlockSpec(memory_space=pltpu.SMEM)] + [vmem] * 8 + [pl.BlockSpec(memory_space=pl.ANY)],
        out_specs=[vmem] * 2,
        scratch_shapes=[pltpu.VMEM((2, 1, 1, tall, LANES), F32)] * 2
        + [strip] * 6
        + [pltpu.VMEM((4, 2, 2, 4 * TILE, LANES), F32)] * 2
        + [pltpu.VMEM((2, 2, 4 * TILE, LANES), F32)]
        + [row] * 5
        + [pltpu.VMEM((2, 2, rows, cols), F32), pltpu.SemaphoreType.DMA((4,))],
        compiler_params=pltpu.CompilerParams(vmem_limit_bytes=24 * MIB),
        name="rim_sums",
    )(core, west, east, from_west, from_east, low, high, south, north, perturb)


def close_kernel(bands, core, *rest):
    count = len(bands)
    parts = [rest[4 * j : 4 * j + 4] for j in range(count)]
    out, buf, sems = rest[4 * count :]
    rim_at = 2 * bands[-1][1]
    rows = buf.shape[1]
    block = rows * TILE // LANES
    lane = lane_ids(TILE)
    row = lax.broadcasted_iota(jnp.int32, (TILE, LANES), 0)
    copies = []
    for who in range(2):
        level = core[0] if who == 0 else 1 - core[0]
        last = parts[-1]
        for j, (low, size) in enumerate(bands):
            one, two = parts[j][2 * who], parts[j][2 * who + 1]
            for q in range(0, size, TILE):
                r = low + q
                g, k = r // block, r % block
                side = last[2 * who][rim_at + k : rim_at + k + TILE, :] + last[2 * who + 1][rim_at + k : rim_at + k + TILE, :]
                for t in range(2):
                    at = t * size + q
                    value = one[at : at + TILE, :] + two[at : at + TILE, :]
                    if r in (0, rows - TILE):
                        ra = rim_at + block + TILE * t
                        ends = last[2 * who][ra : ra + TILE, :] + last[2 * who + 1][ra : ra + TILE, :]
                        value = jnp.where(row < 3 if r == 0 else row >= TILE - 3, ends, value)
                    if t == 0:
                        value = jnp.where(lane < 3, spin(side, -TILE * g), value)
                    else:
                        value = jnp.where(lane >= LANES - 3, spin(side, LANES - 8 - TILE * g), value)
                    buf[who, r : r + TILE, t * LANES : (t + 1) * LANES] = value
            span = pl.ds(low, size)
            copy = pltpu.make_async_copy(buf.at[who, span], out.at[level, span], sems.at[who * count + j])
            copy.start()
            copies.append(copy)
    finish(copies)


def close(bands, core, parts, rows, cols):
    vmem = pl.BlockSpec(memory_space=pltpu.VMEM)
    flat = [value for part in parts for value in part]
    return pl.pallas_call(
        functools.partial(close_kernel, bands),
        out_shape=jax.ShapeDtypeStruct((2, rows, cols), F32),
        in_specs=[pl.BlockSpec(memory_space=pltpu.SMEM)] + [vmem] * len(flat),
        out_specs=pl.BlockSpec(memory_space=pl.ANY),
        scratch_shapes=[pltpu.VMEM((2, rows, cols), F32), pltpu.SemaphoreType.DMA((2 * len(bands),))],
        compiler_params=pltpu.CompilerParams(vmem_limit_bytes=24 * MIB),
        name="close",
    )(core, *flat)


def per_device(perturb, control, diffusivity, sea_mask, fold_partner):
    rows, cols = diffusivity.shape
    lon_count, lat_count = lax.axis_size("lon"), lax.axis_size("lat")
    lat = lax.axis_index("lat")
    start = fold_partner[0]
    core = (lax.axis_index("mem") % 2).astype(jnp.int32).reshape(1)
    place = jnp.stack([lat.astype(jnp.int32), start % cols])
    swap = functools.partial(lax.ppermute, axis_name="mem", perm=[(i, i ^ 1) for i in range(4)])
    across = functools.partial(lax.ppermute, axis_name="mem", perm=[(i, i ^ 2) for i in range(4)])
    size = rows // 4
    bands = [(i * size, size) for i in range(4)]
    args = (core, control, perturb, diffusivity, sea_mask)

    low, high, message = edges(place, control, diffusivity, sea_mask)
    low_rows = lax.ppermute(message, "lat", [(0, 1), (1, 0)])

    def folded(a):
        def branch(value):
            return tuple(
                lax.ppermute(
                    value,
                    ("lon", "lat"),
                    [((a - n - i) % lon_count * lat_count + 1, i * lat_count + 1) for i in range(lon_count)],
                )
                for n in range(2)
            )

        return branch

    fold_a, fold_b = lax.switch(start // cols, [folded(a) for a in range(lon_count)], high)
    west, east, to_east, to_west, south, north = pack_strips(
        place, control, diffusivity, sea_mask, low_rows, fold_a, fold_b
    )
    from_west = lax.ppermute(to_east, "lon", [(i, (i + 1) % lon_count) for i in range(lon_count)])
    from_east = lax.ppermute(to_west, "lon", [(i, (i - 1) % lon_count) for i in range(lon_count)])
    rim_keep, rim_send = rim_sums(core, west, east, from_west, from_east, low, high, south, north, perturb)

    parts = []
    for j, (at, count) in enumerate(bands):
        last = j == len(bands) - 1
        other = swap(band(False, at, count, *args, rim=rim_send if last else None))
        mine = band(True, at, count, *args, rim=rim_keep if last else None, other=other)
        far = across(mine)
        parts.append((mine, far, swap(mine), swap(far)))
    return close(bands, core, parts, rows, cols)


def solution(mesh):
    return jax.shard_map(
        per_device,
        mesh=mesh,
        in_specs=(
            P("mem", None, "lat", "lon"),
            P("mem", None, "lat", "lon"),
            P("lat", "lon"),
            P(None, "lat", "lon"),
            P(),
        ),
        out_specs=P(None, "lat", "lon"),
        check_vma=False,
    )
```
